32 devices in a mesh: grp: 8 (over z, x), loc: 4 (over y, core).
Axes of the slice: x: 2, y: 2, z: 4, core: 2. Of those that a mesh axis runs over, the one named last changes fastest.
Arguments:
- acts: bfloat16 [4096, 2048], P(('grp', 'loc')), may hold values from -6 to 6
- out_grad: bfloat16 [4096, 2048], P(('grp', 'loc')), may hold values from -6 to 6
- expert_ids: int32 [4096, 8], P(('grp', 'loc')), may hold values from 0 to 31, all different within a row; in each aligned block of 128 rows (0 to 127, 128 to 255, ...) at most 36 rows name the same one
- gate_vals: bfloat16 [4096, 8], P(('grp', 'loc')), may hold values from 0.049804688 to 0.5
- w_gate: bfloat16 [32, 2048, 768], P(('grp', 'loc')), may hold values from -0.125 to 0.125
- w_up: bfloat16 [32, 2048, 768], P(('grp', 'loc')), may hold values from -0.125 to 0.125
- w_down: bfloat16 [32, 768, 2048], P(('grp', 'loc')), may hold values from -0.21875 to 0.21875
Outputs:
- grad_acts: bfloat16 [4096, 2048], P(('grp', 'loc'))
- grad_gates: bfloat16 [4096, 8], P(('grp', 'loc'))
- grad_w_gate: bfloat16 [32, 2048, 768], P(('grp', 'loc'))
- grad_w_up: bfloat16 [32, 2048, 768], P(('grp', 'loc'))
- grad_w_down: bfloat16 [32, 768, 2048], P(('grp', 'loc'))
The draws below stay inside these ranges and needn't reach their ends.
Inputs may be any that keep to these rules, and one draw needn't show every extreme that they name: `expert_ids`: each token names 8 different experts. Among the 128 tokens of one device, no expert is named by more than 36 of them, and in every draw some expert is named by exactly 36 of one device's tokens.
All inputs are finite; a program needn't handle non-finite values.
Results may differ from the reference program's by a relative error of at most 0.0058.
Values may be sent and summed in bfloat16 or wider, within the bound.
A program may use at most 128 MiB of HBM per device.

```python
import math
import jax
import jax.numpy as jnp
import numpy as np
from jax import lax

D = 2048
FF = 768
TOPK = 8
T_DEV = 128
EXPERTS = 32
CAP = 36
TOKENS = 4096
N_GRP = 8
N_LOC = 4


def shard_levels(stream_key, extent, split, least, top_value):
    factor_of, own = 1.0, jax.random.fold_in(stream_key, 6)
    for dim, blocks in split:
        heights = jnp.exp(jax.random.uniform(jax.random.fold_in(own, dim), (blocks,), jnp.float32, least / len(split), top_value / len(split)))
        factor_of = factor_of * jnp.repeat(heights, extent[dim] // blocks).reshape([-1 if axis == dim else 1 for axis in range(len(extent))])
    return factor_of


def routed_block(rng, own, number, rows, count, top, most, skew):
    sequence = jax.random.permutation(rng, count)
    packed, ordinary = load_shares(count, rows * top, most, skew, True), load_shares(count, rows * top, most, skew, False)
    places = jnp.arange(count)

    def named(sizes, rotation):
        used = int((sizes > 0).sum())
        fixed = max(1, used // 4)
        passed = fixed + (places - fixed + rotation * (used - fixed)) % max(1, count - fixed)
        return jnp.zeros((count,), jnp.int32).at[sequence[jnp.where(places < fixed, places, passed)]].set(jnp.asarray(sizes, jnp.int32))

    sizes = jnp.where(number % 4 == 0, named(packed, number // 4), named(ordinary, number - number // 4 - 1))
    mixed = jax.random.permutation(jax.random.fold_in(own, 3), count)
    giver, sink = mixed[0:count // 2 * 2:2], mixed[1:count // 2 * 2:2]
    room = jnp.minimum(sizes[giver] - 1, most - sizes[sink]) // 2
    room = jnp.where((giver == sequence[0]) | (sink == sequence[0]) | (sizes[sink] == 0), 0, jnp.maximum(room, 0))
    passed = jax.random.randint(jax.random.fold_in(own, 4), (count // 2,), 0, 1 << 20) % (room + 1)
    sizes = sizes.at[giver].add(-passed).at[sink].add(passed)
    members = jnp.searchsorted(jnp.cumsum(sizes), jnp.arange(rows * top), side="right").astype(jnp.int32)
    listing = members.reshape(top, rows).T
    listing = listing[jax.random.permutation(jax.random.fold_in(own, 1), rows)]
    rotation = jax.random.randint(jax.random.fold_in(own, 2), (rows, 1), 0, top)
    return jnp.take_along_axis(listing, (jnp.arange(top)[None, :] + rotation) % top, axis=1)


def load_shares(amount, total, reach, lean, full):
    portions = [(1 << 20) // math.isqrt(rank ** lean) + 1 for rank in range(1, amount + 1)]
    largest = reach if full else min(reach, max(-(-total // amount), total * portions[0] // sum(portions)))
    least = 1 if total - largest >= amount - 1 else 0
    counts, rest = [largest] + [least] * (amount - 1), total - largest - least * (amount - 1)
    while rest > 0:
        free = [i for i in range(1, amount) if counts[i] < largest] or [i for i in range(1, amount) if counts[i] < reach]
        mass, remaining = sum([portions[i] for i in free]), rest
        for i in free:
            more = min(reach - counts[i], max(1, remaining * portions[i] // mass), rest)
            counts[i] = counts[i] + more
            rest = rest - more
    return np.array(counts)


def bell_draw(stream_key, shape, scale, bound, shards=(), kind=jnp.bfloat16):
    values = scale * jax.random.normal(stream_key, shape, jnp.float32)
    if shards:
        values = values * shard_levels(stream_key, shape, shards, -0.22, 0.18)
    return jnp.clip(values, -bound, bound).astype(kind)


def setup_inputs(seed: int = 0) -> dict:
    arg_keys = jax.random.split(jax.random.key(seed), 8)
    acts = bell_draw(arg_keys[0], (TOKENS, D), 1.0, 6.0, ((0, 32),))
    out_grad = bell_draw(arg_keys[1], (TOKENS, D), 1.0, 6.0, ((0, 32),))
    expert_ids_keys = jax.random.split(jax.random.fold_in(arg_keys[2], 1), TOKENS // T_DEV)
    expert_ids_turns = jax.random.permutation(jax.random.fold_in(arg_keys[2], 3), TOKENS // T_DEV)
    expert_ids = jax.vmap(lambda own, number: routed_block(jax.random.fold_in(arg_keys[2], 2), own, number, T_DEV, EXPERTS, TOPK, CAP, 2))(expert_ids_keys, expert_ids_turns).reshape((TOKENS, TOPK))
    gate_vals = jnp.clip(jnp.exp(math.log(0.5) - 2.306499 * jax.random.uniform(arg_keys[3], (TOKENS, TOPK), jnp.float32) ** shard_levels(arg_keys[3], (TOKENS, TOPK), ((0, 32),), -0.2, 0.2)), 0.049804688, 0.5).astype(jnp.bfloat16)
    w_gate = bell_draw(arg_keys[4], (EXPERTS, D, FF), D ** -0.5, 0.125, ((0, 32),))
    w_up = bell_draw(arg_keys[5], (EXPERTS, D, FF), D ** -0.5, 0.125, ((0, 32),))
    w_down = bell_draw(arg_keys[6], (EXPERTS, FF, D), FF ** -0.5, 0.21875, ((0, 32),))
    return {"acts": acts, "out_grad": out_grad, "expert_ids": expert_ids, "gate_vals": gate_vals, "w_gate": w_gate, "w_up": w_up, "w_down": w_down}


def contract(left, right, left_dim, right_dim):
    return lax.dot_general(left, right, (((left_dim,), (right_dim,)), ((), ())), preferred_element_type=jnp.float32)


def expert_grads(rows_in, rows_grad, rows_gate, wg_one, wu_one, wd_one):
    gate_pre = jnp.dot(rows_in, wg_one, preferred_element_type=jnp.float32)
    up_proj = jnp.dot(rows_in, wu_one, preferred_element_type=jnp.float32)
    sigmoid_gate = jax.nn.sigmoid(gate_pre)
    activated = gate_pre * sigmoid_gate
    hidden = activated * up_proj
    dh_raw = contract(rows_grad, wd_one, 1, 1)
    gate_grad = jnp.sum(hidden * dh_raw, axis=1).astype(jnp.bfloat16)
    weight_col = rows_gate.astype(jnp.float32)[:, None]
    scaled_hidden = (weight_col * hidden).astype(jnp.bfloat16)
    down_grad = contract(scaled_hidden, rows_grad, 0, 0).astype(jnp.bfloat16)
    hidden_grad = weight_col * dh_raw
    pre_grad = (hidden_grad * up_proj * sigmoid_gate * (1.0 + gate_pre * (1.0 - sigmoid_gate))).astype(jnp.bfloat16)
    up_grad = (hidden_grad * activated).astype(jnp.bfloat16)
    wg_grad = contract(rows_in, pre_grad, 0, 0).astype(jnp.bfloat16)
    wu_grad = contract(rows_in, up_grad, 0, 0).astype(jnp.bfloat16)
    input_grad = (contract(pre_grad, wg_one, 1, 1) + contract(up_grad, wu_one, 1, 1)).astype(jnp.bfloat16)
    return input_grad, gate_grad, wg_grad, wu_grad, down_grad


def device_sources(dev_ids):
    flat_ids = dev_ids.reshape(-1)
    one_hot = (flat_ids[:, None] == jnp.arange(EXPERTS, dtype=jnp.int32)[None, :]).astype(jnp.int32)
    before = jnp.cumsum(one_hot, axis=0) - one_hot
    rank_in = jnp.sum(before * one_hot, axis=1)
    slot_of = flat_ids * CAP + rank_in
    entries = T_DEV * TOPK
    return jnp.full((EXPERTS * CAP,), entries, jnp.int32).at[slot_of].set(jnp.arange(entries, dtype=jnp.int32))


def reference(acts, out_grad, expert_ids, gate_vals, w_gate, w_up, w_down):
    devices = N_GRP * N_LOC
    entries = T_DEV * TOPK
    sources = jax.vmap(device_sources)(expert_ids.reshape(devices, T_DEV, TOPK))
    padded_acts = jnp.concatenate([acts, jnp.zeros((1, D), acts.dtype)], axis=0)
    padded_grad = jnp.concatenate([out_grad, jnp.zeros((1, D), out_grad.dtype)], axis=0)
    padded_gate = jnp.concatenate([gate_vals.reshape(-1), jnp.zeros((1,), gate_vals.dtype)], axis=0)
    dev_base = jnp.arange(devices, dtype=jnp.int32)[:, None]

    def one_expert(carry, expert):
        acc_rows, acc_gate = carry
        cols = lax.dynamic_slice_in_dim(sources, expert * CAP, CAP, 1)
        valid = cols < entries
        row_index = jnp.where(valid, dev_base * T_DEV + cols // TOPK, TOKENS).reshape(-1).astype(jnp.int32)
        gate_index = jnp.where(valid, dev_base * entries + cols, TOKENS * TOPK).reshape(-1).astype(jnp.int32)
        input_grad, gate_grad, wg_grad, wu_grad, down_grad = expert_grads(
            padded_acts[row_index], padded_grad[row_index], padded_gate[gate_index],
            w_gate[expert], w_up[expert], w_down[expert])
        acc_rows = acc_rows.at[row_index].add(input_grad.astype(jnp.float32))
        acc_gate = acc_gate.at[gate_index].set(gate_grad.astype(jnp.float32))
        return (acc_rows, acc_gate), (wg_grad, wu_grad, down_grad)

    start = (jnp.zeros((TOKENS + 1, D), jnp.float32), jnp.zeros((TOKENS * TOPK + 1,), jnp.float32))
    (acc_rows, acc_gate), (grad_w_gate, grad_w_up, grad_w_down) = lax.scan(
        one_expert, start, jnp.arange(EXPERTS, dtype=jnp.int32))
    grad_acts = acc_rows[:TOKENS].astype(jnp.bfloat16)
    grad_gates = acc_gate[:TOKENS * TOPK].reshape(TOKENS, TOPK).astype(jnp.bfloat16)
    return grad_acts, grad_gates, grad_w_gate, grad_w_up, grad_w_down
```

```python
import jax
import jax.numpy as jnp
from jax import lax
from jax.sharding import Mesh, PartitionSpec as P

PLANE = ("x", "loc")


def contract(left, right, left_dim, right_dim):
    return lax.dot_general(
        left, right, (((left_dim,), (right_dim,)), ((), ())), preferred_element_type=jnp.float32
    )


def exchange(rows, axes):
    return lax.all_to_all(rows, axes, split_axis=0, concat_axis=0, tiled=True)


def body(acts, out_grad, expert_ids, gate_vals, w_gate, w_up, w_down):
    tokens, width = acts.shape
    top_count = expert_ids.shape[1]
    n_z = lax.axis_size("z")
    n_plane = lax.axis_size("x") * lax.axis_size("loc")
    capacity = 9 * tokens * top_count // (8 * n_z * n_plane)
    rows = n_z * capacity
    count = n_z * tokens
    wg_one, wu_one, wd_one = w_gate[0], w_up[0], w_down[0]

    ids = lax.all_gather(expert_ids, "z", axis=0, tiled=True)
    gates = lax.all_gather(gate_vals, "z", axis=0, tiled=True)
    col_acts = lax.all_gather(acts, "z", axis=0, tiled=True)
    col_grad = lax.all_gather(out_grad, "z", axis=0, tiled=True)

    first = lax.axis_index("z") * n_plane
    hit = ids[:, None, :] == first + jnp.arange(n_plane, dtype=jnp.int32)[None, :, None]
    member = jnp.any(hit, axis=2)
    gate_of = jnp.sum(jnp.where(hit, gates[:, None, :].astype(jnp.float32), 0.0), axis=2)
    order = jnp.arange(count, dtype=jnp.int32)
    earlier = (order[:, None] > order[None, :]).astype(jnp.bfloat16)
    rank = jnp.dot(earlier, member.astype(jnp.bfloat16), preferred_element_type=jnp.float32)
    slot = jnp.where(member, rank.astype(jnp.int32), -1).T
    chosen = slot[:, None, :] == jnp.arange(rows, dtype=jnp.int32)[None, :, None]
    pick = chosen.astype(jnp.bfloat16).reshape(n_plane * rows, count)
    send_gate = jnp.sum(jnp.where(chosen, gate_of.T[:, None, :], 0.0), axis=2)

    send_acts = contract(pick, col_acts, 1, 0).astype(jnp.bfloat16)
    rows_in = exchange(send_acts, PLANE)
    rows_gate = exchange(send_gate.astype(jnp.bfloat16), PLANE).reshape(-1)
    send_grad = contract(pick, col_grad, 1, 0).astype(jnp.bfloat16)
    rows_grad = exchange(send_grad, PLANE)

    gate_pre = jnp.dot(rows_in, wg_one, preferred_element_type=jnp.float32)
    up_proj = jnp.dot(rows_in, wu_one, preferred_element_type=jnp.float32)
    sigmoid_gate = jax.nn.sigmoid(gate_pre)
    activated = gate_pre * sigmoid_gate
    hidden = activated * up_proj
    dh_raw = contract(rows_grad, wd_one, 1, 1)
    gate_grad = jnp.sum(hidden * dh_raw, axis=1).astype(jnp.bfloat16)
    weight_col = rows_gate.astype(jnp.float32)[:, None]
    scaled_hidden = (weight_col * hidden).astype(jnp.bfloat16)
    hidden_grad = weight_col * dh_raw
    pre_grad = (
        hidden_grad * up_proj * sigmoid_gate * (1.0 + gate_pre * (1.0 - sigmoid_gate))
    ).astype(jnp.bfloat16)
    up_grad = (hidden_grad * activated).astype(jnp.bfloat16)
    input_grad = (contract(pre_grad, wg_one, 1, 1) + contract(up_grad, wu_one, 1, 1)).astype(
        jnp.bfloat16
    )
    back_rows = exchange(input_grad, PLANE)
    back_gate = exchange(gate_grad.reshape(n_plane, rows), PLANE)

    down_grad = contract(scaled_hidden, rows_grad, 0, 0).astype(jnp.bfloat16)
    wg_grad = contract(rows_in, pre_grad, 0, 0).astype(jnp.bfloat16)
    wu_grad = contract(rows_in, up_grad, 0, 0).astype(jnp.bfloat16)

    partial = contract(pick, back_rows, 0, 0).astype(jnp.bfloat16)
    planes = exchange(partial, "z").reshape(n_z, tokens, width)
    grad_acts = jnp.sum(planes.astype(jnp.float32), axis=0).astype(jnp.bfloat16)

    gate_part = jnp.sum(
        jnp.where(chosen, back_gate.astype(jnp.float32)[:, :, None], 0.0), axis=1
    ).T.astype(jnp.bfloat16)
    gate_all = exchange(gate_part, "z").reshape(n_z, tokens, n_plane)
    gate_all = gate_all.transpose(1, 0, 2).reshape(tokens, n_z * n_plane)
    named = expert_ids[:, :, None] == jnp.arange(n_z * n_plane, dtype=jnp.int32)[None, None, :]
    grad_gates = jnp.sum(
        jnp.where(named, gate_all.astype(jnp.float32)[:, None, :], 0.0), axis=2
    ).astype(jnp.bfloat16)
    return (grad_acts, grad_gates, wg_grad[None], wu_grad[None], down_grad[None])


def solution(mesh):
    n_group, n_local = mesh.shape["grp"], mesh.shape["loc"]
    n_z = 1
    while n_z * n_z < n_group:
        n_z *= 2
    if n_group % n_z:
        n_z = n_group
    cube = Mesh(mesh.devices.reshape(n_z, n_group // n_z, n_local), ("z", "x", "loc"))
    whole = ("z", "x", "loc")
    two, three = P(whole, None), P(whole, None, None)
    return jax.shard_map(
        body,
        mesh=cube,
        in_specs=(two, two, two, two, three, three, three),
        out_specs=(two, two, three, three, three),
        check_vma=False,
    )
```

```python
import jax
import jax.numpy as jnp
from jax import lax
from jax.sharding import Mesh, PartitionSpec as P

PLANE = ("x", "loc")
ACTS_CUTS = 2
GRAD_CUTS = 2


def cut(array, parts):
    return jnp.split(array, parts, axis=1)


def contract(left, right, left_dim, right_dim):
    return lax.dot_general(
        left, right, (((left_dim,), (right_dim,)), ((), ())), preferred_element_type=jnp.float32
    )


def exchange(rows, axes):
    return lax.all_to_all(rows, axes, split_axis=0, concat_axis=0, tiled=True)


def shifted(block, step):
    n_z = lax.axis_size("z")
    return lax.ppermute(block, "z", [(i, (i + step) % n_z) for i in range(n_z)])


def column(block):
    blocks = [block] + [shifted(block, j) for j in range(1, lax.axis_size("z"))]
    return jnp.concatenate(blocks, axis=0)


def body(acts, out_grad, expert_ids, gate_vals, w_gate, w_up, w_down):
    tokens, width = acts.shape
    top_count = expert_ids.shape[1]
    n_z = lax.axis_size("z")
    n_plane = lax.axis_size("x") * lax.axis_size("loc")
    capacity = 9 * tokens * top_count // (8 * n_z * n_plane)
    rows = n_z * capacity
    count = n_z * tokens
    wg_one, wu_one, wd_one = w_gate[0], w_up[0], w_down[0]

    small = jnp.concatenate([expert_ids.astype(jnp.float32), gate_vals.astype(jnp.float32)], axis=1)
    small = column(small)
    ids = small[:, :top_count].astype(jnp.int32)
    gates = small[:, top_count:]
    half = width // 2

    acts_parts = [column(part) for part in cut(acts, ACTS_CUTS)]
    out_grad, *acts_parts = lax.optimization_barrier((out_grad, *acts_parts))
    grad_parts = [column(part) for part in cut(out_grad, GRAD_CUTS)]

    first = lax.axis_index("z") * n_plane
    hit = ids[:, None, :] == first + jnp.arange(n_plane, dtype=jnp.int32)[None, :, None]
    member = jnp.any(hit, axis=2)
    gate_of = jnp.sum(jnp.where(hit, gates[:, None, :], 0.0), axis=2)
    order = jnp.arange(count, dtype=jnp.int32)
    earlier = (order[:, None] > order[None, :]).astype(jnp.bfloat16)
    rank = jnp.dot(earlier, member.astype(jnp.bfloat16), preferred_element_type=jnp.float32)
    slot = jnp.where(member, rank.astype(jnp.int32), -1).T
    chosen = slot[:, None, :] == jnp.arange(rows, dtype=jnp.int32)[None, :, None]
    pick = chosen.astype(jnp.bfloat16).reshape(n_plane * rows, count)

    lanes = -(-n_plane // 128) * 128
    gate_cols = jnp.pad(gate_of, ((0, 0), (0, lanes - n_plane))).astype(jnp.bfloat16)
    grad_parts[-1] = jnp.concatenate([grad_parts[-1], gate_cols], axis=1)

    in_parts = [
        exchange(contract(pick, part, 1, 0).astype(jnp.bfloat16), PLANE) for part in acts_parts
    ]
    got_parts = [
        exchange(contract(pick, part, 1, 0).astype(jnp.bfloat16), PLANE) for part in grad_parts
    ]
    place = lax.axis_index("x") * lax.axis_size("loc") + lax.axis_index("loc")
    mine = jnp.arange(lanes, dtype=jnp.int32)[None, :] == place
    last = width // GRAD_CUTS
    weight_col = jnp.sum(
        jnp.where(mine, got_parts[-1][:, last:].astype(jnp.float32), 0.0), axis=1, keepdims=True
    )
    got_parts[-1] = got_parts[-1][:, :last]
    rows_in = jnp.concatenate(in_parts, axis=1)
    rows_grad = jnp.concatenate(got_parts, axis=1)

    gate_pre = sum(
        jnp.dot(part, weight, preferred_element_type=jnp.float32)
        for part, weight in zip(in_parts, jnp.split(wg_one, ACTS_CUTS, axis=0))
    )
    up_proj = sum(
        jnp.dot(part, weight, preferred_element_type=jnp.float32)
        for part, weight in zip(in_parts, jnp.split(wu_one, ACTS_CUTS, axis=0))
    )
    sigmoid_gate = jax.nn.sigmoid(gate_pre)
    activated = gate_pre * sigmoid_gate
    hidden = activated * up_proj
    dh_raw = sum(
        contract(part, weight, 1, 1)
        for part, weight in zip(got_parts, jnp.split(wd_one, GRAD_CUTS, axis=1))
    )
    gate_grad = jnp.sum(hidden * dh_raw, axis=1).astype(jnp.bfloat16)
    scaled_hidden = (weight_col * hidden).astype(jnp.bfloat16)
    hidden_grad = weight_col * dh_raw
    pre_grad = (
        hidden_grad * up_proj * sigmoid_gate * (1.0 + gate_pre * (1.0 - sigmoid_gate))
    ).astype(jnp.bfloat16)
    up_grad = (hidden_grad * activated).astype(jnp.bfloat16)

    def input_grad(low, high):
        return (
            contract(pre_grad, wg_one[low:high], 1, 1) + contract(up_grad, wu_one[low:high], 1, 1)
        ).astype(jnp.bfloat16)

    experts = n_z * n_plane
    wide = -(-experts // 128) * 128
    own = jnp.arange(wide, dtype=jnp.int32)[None, :] == first + place
    gate_lane = jnp.where(own, gate_grad[:, None], jnp.zeros((), jnp.bfloat16))
    dx_a = input_grad(0, half)
    dx_b = jnp.concatenate([input_grad(half, width), gate_lane], axis=1)
    back_a = exchange(dx_a, PLANE)
    dx_b, pre_late, up_late, hidden_late = lax.optimization_barrier(
        (dx_b, pre_grad, up_grad, scaled_hidden)
    )
    back_b = exchange(dx_b, PLANE)

    down_grad = contract(hidden_late, rows_grad, 0, 0).astype(jnp.bfloat16)
    wg_grad = contract(rows_in, pre_late, 0, 0).astype(jnp.bfloat16)
    back_a, down_grad = lax.optimization_barrier((back_a, down_grad))

    def over_planes(back):
        planes = contract(pick, back, 0, 0).astype(jnp.bfloat16)
        planes = planes.reshape(n_z, tokens, back.shape[1])
        total = planes[0].astype(jnp.float32)
        for j in range(1, n_z):
            total = total + shifted(planes[j], n_z - j).astype(jnp.float32)
        return total.astype(jnp.bfloat16)

    sum_a = over_planes(back_a)
    wu_grad = contract(rows_in, up_late, 0, 0).astype(jnp.bfloat16)
    back_b, wg_grad, wu_grad = lax.optimization_barrier((back_b, wg_grad, wu_grad))
    sum_b = over_planes(back_b)
    grad_acts = jnp.concatenate([sum_a, sum_b[:, : width - half]], axis=1)
    gate_all = sum_b[:, width - half :].astype(jnp.float32)
    named = expert_ids[:, :, None] == jnp.arange(wide, dtype=jnp.int32)[None, None, :]
    grad_gates = jnp.sum(jnp.where(named, gate_all[:, None, :], 0.0), axis=2).astype(jnp.bfloat16)
    return (grad_acts, grad_gates, wg_grad[None], wu_grad[None], down_grad[None])


def solution(mesh):
    n_group, n_local = mesh.shape["grp"], mesh.shape["loc"]
    n_z = 1
    while n_z * n_z < n_group:
        n_z *= 2
    if n_group % n_z:
        n_z = n_group
    cube = Mesh(mesh.devices.reshape(n_z, n_group // n_z, n_local), ("z", "x", "loc"))
    whole = ("z", "x", "loc")
    two, three = P(whole, None), P(whole, None, None)
    return jax.shard_map(
        body,
        mesh=cube,
        in_specs=(two, two, two, two, three, three, three),
        out_specs=(two, two, three, three, three),
        check_vma=False,
    )
```

```python
import jax
import jax.numpy as jnp
from jax import lax
from jax.sharding import Mesh, PartitionSpec as P

PLANE = ("x", "loc")
ACTS_CUTS = 2
GRAD_CUTS = 2


def cut(array, parts):
    return jnp.split(array, parts, axis=1)


def contract(left, right, left_dim, right_dim):
    return lax.dot_general(
        left, right, (((left_dim,), (right_dim,)), ((), ())), preferred_element_type=jnp.float32
    )


def exchange(rows, axes):
    return lax.all_to_all(rows, axes, split_axis=0, concat_axis=0, tiled=True)


def shifted(block, step):
    n_z = lax.axis_size("z")
    return lax.ppermute(block, "z", [(i, (i + step) % n_z) for i in range(n_z)])


def column(block):
    blocks = [block] + [shifted(block, j) for j in range(1, lax.axis_size("z"))]
    return jnp.concatenate(blocks, axis=0)


def body(acts, out_grad, expert_ids, gate_vals, w_gate, w_up, w_down):
    tokens, width = acts.shape
    top_count = expert_ids.shape[1]
    n_z = lax.axis_size("z")
    n_plane = lax.axis_size("x") * lax.axis_size("loc")
    capacity = 9 * tokens * top_count // (8 * n_z * n_plane)
    rows = n_z * capacity
    count = n_z * tokens
    wg_one, wu_one, wd_one = w_gate[0], w_up[0], w_down[0]

    small = jnp.concatenate([expert_ids.astype(jnp.float32), gate_vals.astype(jnp.float32)], axis=1)
    small = column(small)
    ids = small[:, :top_count].astype(jnp.int32)
    gates = small[:, top_count:]
    half = width // 2

    acts_parts = [column(part) for part in cut(acts, ACTS_CUTS)]
    out_grad, *acts_parts = lax.optimization_barrier((out_grad, *acts_parts))
    grad_parts = [column(part) for part in cut(out_grad, GRAD_CUTS)]

    parts = acts_parts + grad_parts
    for i in range(1, len(parts) - 1):
        parts[i], parts[i + 1] = lax.optimization_barrier((parts[i], parts[i + 1]))
    acts_parts, grad_parts = parts[:ACTS_CUTS], parts[ACTS_CUTS:]

    first = lax.axis_index("z") * n_plane
    hit = ids[:, None, :] == first + jnp.arange(n_plane, dtype=jnp.int32)[None, :, None]
    member = jnp.any(hit, axis=2)
    gate_of = jnp.sum(jnp.where(hit, gates[:, None, :], 0.0), axis=2)
    order = jnp.arange(count, dtype=jnp.int32)
    earlier = (order[:, None] > order[None, :]).astype(jnp.bfloat16)
    rank = jnp.dot(earlier, member.astype(jnp.bfloat16), preferred_element_type=jnp.float32)
    slot = jnp.where(member, rank.astype(jnp.int32), -1).T
    chosen = slot[:, None, :] == jnp.arange(rows, dtype=jnp.int32)[None, :, None]
    pick = chosen.astype(jnp.bfloat16).reshape(n_plane * rows, count)

    lanes = -(-n_plane // 128) * 128
    gate_cols = jnp.pad(gate_of, ((0, 0), (0, lanes - n_plane))).astype(jnp.bfloat16)
    grad_parts[-1] = jnp.concatenate([grad_parts[-1], gate_cols], axis=1)

    in_parts = [
        exchange(contract(pick, part, 1, 0).astype(jnp.bfloat16), PLANE) for part in acts_parts
    ]
    got_parts = [
        exchange(contract(pick, part, 1, 0).astype(jnp.bfloat16), PLANE) for part in grad_parts
    ]
    place = lax.axis_index("x") * lax.axis_size("loc") + lax.axis_index("loc")
    mine = jnp.arange(lanes, dtype=jnp.int32)[None, :] == place
    last = width // GRAD_CUTS
    weight_col = jnp.sum(
        jnp.where(mine, got_parts[-1][:, last:].astype(jnp.float32), 0.0), axis=1, keepdims=True
    )
    got_parts[-1] = got_parts[-1][:, :last]
    rows_in = jnp.concatenate(in_parts, axis=1)
    rows_grad = jnp.concatenate(got_parts, axis=1)

    gate_pre = sum(
        jnp.dot(part, weight, preferred_element_type=jnp.float32)
        for part, weight in zip(in_parts, jnp.split(wg_one, ACTS_CUTS, axis=0))
    )
    up_proj = sum(
        jnp.dot(part, weight, preferred_element_type=jnp.float32)
        for part, weight in zip(in_parts, jnp.split(wu_one, ACTS_CUTS, axis=0))
    )
    sigmoid_gate = jax.nn.sigmoid(gate_pre)
    activated = gate_pre * sigmoid_gate
    hidden = activated * up_proj
    dh_raw = sum(
        contract(part, weight, 1, 1)
        for part, weight in zip(got_parts, jnp.split(wd_one, GRAD_CUTS, axis=1))
    )
    gate_grad = jnp.sum(hidden * dh_raw, axis=1).astype(jnp.bfloat16)
    scaled_hidden = (weight_col * hidden).astype(jnp.bfloat16)
    hidden_grad = weight_col * dh_raw
    pre_grad = (
        hidden_grad * up_proj * sigmoid_gate * (1.0 + gate_pre * (1.0 - sigmoid_gate))
    ).astype(jnp.bfloat16)
    up_grad = (hidden_grad * activated).astype(jnp.bfloat16)

    def input_grad(low, high):
        return (
            contract(pre_grad, wg_one[low:high], 1, 1) + contract(up_grad, wu_one[low:high], 1, 1)
        ).astype(jnp.bfloat16)

    experts = n_z * n_plane
    wide = -(-experts // 128) * 128
    own = jnp.arange(wide, dtype=jnp.int32)[None, :] == first + place
    gate_lane = jnp.where(own, gate_grad[:, None], jnp.zeros((), jnp.bfloat16))
    dx_a = input_grad(0, half)
    dx_b = jnp.concatenate([input_grad(half, width), gate_lane], axis=1)
    back_a = exchange(dx_a, PLANE)
    dx_b, pre_late, up_late, hidden_late = lax.optimization_barrier(
        (dx_b, pre_grad, up_grad, scaled_hidden)
    )
    back_b = exchange(dx_b, PLANE)

    down_grad = contract(hidden_late, rows_grad, 0, 0).astype(jnp.bfloat16)
    wg_grad = contract(rows_in, pre_late, 0, 0).astype(jnp.bfloat16)
    back_a, down_grad = lax.optimization_barrier((back_a, down_grad))

    def over_planes(back):
        planes = contract(pick, back, 0, 0).astype(jnp.bfloat16)
        planes = planes.reshape(n_z, tokens, back.shape[1])
        total = planes[0].astype(jnp.float32)
        for j in range(1, n_z):
            total = total + shifted(planes[j], n_z - j).astype(jnp.float32)
        return total.astype(jnp.bfloat16)

    sum_a = over_planes(back_a)
    wu_grad = contract(rows_in, up_late, 0, 0).astype(jnp.bfloat16)
    back_b, wg_grad, wu_grad = lax.optimization_barrier((back_b, wg_grad, wu_grad))
    sum_b = over_planes(back_b)
    grad_acts = jnp.concatenate([sum_a, sum_b[:, : width - half]], axis=1)
    gate_all = sum_b[:, width - half :].astype(jnp.float32)
    named = expert_ids[:, :, None] == jnp.arange(wide, dtype=jnp.int32)[None, None, :]
    grad_gates = jnp.sum(jnp.where(named, gate_all[:, None, :], 0.0), axis=2).astype(jnp.bfloat16)
    return (grad_acts, grad_gates, wg_grad[None], wu_grad[None], down_grad[None])


def solution(mesh):
    n_group, n_local = mesh.shape["grp"], mesh.shape["loc"]
    n_z = 1
    while n_z * n_z < n_group:
        n_z *= 2
    if n_group % n_z:
        n_z = n_group
    cube = Mesh(mesh.devices.reshape(n_z, n_group // n_z, n_local), ("z", "x", "loc"))
    whole = ("z", "x", "loc")
    two, three = P(whole, None), P(whole, None, None)
    return jax.shard_map(
        body,
        mesh=cube,
        in_specs=(two, two, two, two, three, three, three),
        out_specs=(two, two, three, three, three),
        check_vma=False,
    )
```
